32 devices in a mesh: expert: 4 (over y, x), fsdp: 8 (over z, core).
Axes of the slice: x: 2, y: 2, z: 4, core: 2. Of those that a mesh axis runs over, the one named last changes fastest.
Arguments:
- tokens: bfloat16 [1024, 6144], P('fsdp', 'expert'), may hold values from -6 to 6
- cotangent: bfloat16 [1024, 6144], P('fsdp', 'expert'), may hold values from -6 to 6
- routed_experts: int32 [1024, 2], replicated, may hold values from 0 to 7, as said below
- route_weights: float32 [1024, 2], P('fsdp'), may hold values from 0.25 to 1
- gate_matrix: bfloat16 [6144, 32768], P(None, ('expert', 'fsdp')), may hold values from -0.078125 to 0.078125
- up_matrix: bfloat16 [6144, 32768], P(None, ('expert', 'fsdp')), may hold values from -0.078125 to 0.078125
- down_matrix: bfloat16 [32768, 6144], P(('expert', 'fsdp')), may hold values from -0.09375 to 0.09375
Outputs:
- layer_output: bfloat16 [1024, 6144], P('fsdp', 'expert')
- grad_tokens: bfloat16 [1024, 6144], P('fsdp', 'expert')
- grad_gate: bfloat16 [6144, 32768], P(None, ('expert', 'fsdp'))
- grad_up: bfloat16 [6144, 32768], P(None, ('expert', 'fsdp'))
- grad_down: bfloat16 [32768, 6144], P(('expert', 'fsdp'))
The draws below stay inside these ranges and needn't reach their ends.
Inputs may be any that keep to these rules, and one draw needn't show every extreme that they name: `routed_experts`: each row names two different experts. In every aligned block of 128 rows each expert below 2 is named by at most 16 rows; one of these experts is named by exactly 16 rows in every block, and every expert below 2 is named by exactly 16 rows in at least one block.
All inputs are finite; a program needn't handle non-finite values.
Results may differ from the reference program's by a relative error of at most 0.017.
Values may be sent and summed in bfloat16 or wider, within the bound.
A program may use at most 256 MiB of HBM per device.

```python
import jax
import jax.numpy as jnp
from jax import lax

D = 6144
FF = 16384
EXPERTS = 8
WIN = 2
TOK_GRP = 128
CAP = 16
TOKENS = 1024
ROWS = 128
WFF = 32768
HD = 1024


def draw_routed_experts(key, part):
    groups = TOKENS // TOK_GRP
    keylist = jax.random.split(jax.random.fold_in(key, 7), 7)
    full_expert = jax.random.randint(keylist[0], (), 0, WIN)
    counts = jax.random.randint(keylist[1], (groups, WIN), CAP // 2, CAP + 1)
    peak_block = jax.random.randint(keylist[2], (WIN,), 0, groups)
    block_index = jnp.arange(groups)[:, None]
    expert_index = jnp.arange(WIN)[None, :]
    counts = jnp.where(block_index == peak_block[None, :], CAP, counts)
    counts = jnp.where(expert_index == full_expert, CAP, counts)
    perm_keys = jax.random.split(keylist[3], groups * WIN)
    shuffles = jax.vmap(lambda subkey: jax.random.permutation(subkey, TOK_GRP))(perm_keys)
    row_ranks = jnp.argsort(shuffles, axis=1).reshape(groups, WIN, TOK_GRP)
    inside = row_ranks < counts[:, :, None]
    first_in = inside[:, 0, :].reshape(TOKENS)
    second_in = inside[:, 1, :].reshape(TOKENS)
    spare_count = EXPERTS - WIN
    other_pick = jax.random.randint(keylist[4], (TOKENS,), WIN, EXPERTS)
    other_second = WIN + (other_pick - WIN + jax.random.randint(keylist[5], (TOKENS,), 1, spare_count)) % spare_count
    pick_first = jnp.where(first_in, 0, jnp.where(second_in, 1, other_pick))
    pick_second = jnp.where(first_in & second_in, 1, jnp.where(first_in | second_in, other_pick, other_second))
    swapped = jax.random.randint(keylist[6], (TOKENS,), 0, 2)
    leading = jnp.where(swapped == 1, pick_second, pick_first)
    trailing = jnp.where(swapped == 1, pick_first, pick_second)
    return jnp.stack([leading, trailing], axis=1).astype(jnp.int32)


def with_spikes(drawn, key, source, target, blocks, factor):
    owner, partner = [(jnp.arange(drawn.shape[axis_at]) // (drawn.shape[axis_at] // blocks)).reshape([-1 if axis == axis_at else 1 for axis in range(drawn.ndim)]) for axis_at in (source, target)]
    chosen = jax.random.permutation(key, blocks)[partner]
    strong = (owner == chosen) | (owner == (partner + blocks // 2) % blocks)
    return jnp.where(strong, factor * drawn, drawn)


def block_scale(key, dims, cuts, least, top_value):
    def one(position, blocks):
        draws = jax.random.uniform(jax.random.fold_in(jax.random.fold_in(key, 6), position), (blocks,), jnp.float32, least / len(cuts), top_value / len(cuts))
        return jnp.repeat(jnp.exp(draws), dims[position] // blocks).reshape((-1,) + (1,) * (len(dims) - position - 1))

    loudness = one(*cuts[0])
    for cut in cuts[1:]:
        loudness = loudness * one(*cut)
    return loudness


def centred(key, extent, deviation, reach, shards=(), held_as=jnp.bfloat16):
    values = deviation * jax.random.normal(key, extent, jnp.float32)
    if shards:
        values = values * block_scale(key, extent, shards, -0.22, 0.18)
    return jnp.clip(values, -reach, reach).astype(held_as)


def heavy_noise(key, dims, deviation, most, pieces, heavy, kind=jnp.bfloat16):
    entries = deviation * jax.random.normal(key, dims, jnp.float32)
    if pieces:
        entries = entries * block_scale(key, dims, pieces, -0.22, 0.18)
    return jnp.clip(with_spikes(entries, jax.random.fold_in(key, 3), *heavy), -most, most).astype(kind)


def setup_inputs(seed: int = 0) -> dict:
    arg_keys = jax.random.split(jax.random.key(seed), 8)
    tokens = centred(arg_keys[0], (TOKENS, D), 1.0, 6.0, ((0, 8), (1, 4)))
    cotangent = centred(arg_keys[1], (TOKENS, D), 1.0, 6.0, ((0, 8), (1, 4)))
    routed_experts = draw_routed_experts(jax.random.fold_in(arg_keys[7], 71), 0)
    route_weights = jnp.clip(0.25 + 0.75 * jax.random.uniform(arg_keys[3], (TOKENS, 2), jnp.float32) ** block_scale(arg_keys[3], (TOKENS, 2), ((0, 8),), -0.2, 0.2), 0.25, 1.0)
    gate_matrix = centred(arg_keys[4], (D, WFF), D ** -0.5, 0.078125, ((1, 32),))
    up_matrix = centred(arg_keys[5], (D, WFF), D ** -0.5, 0.078125, ((1, 32),))
    down_matrix = heavy_noise(arg_keys[6], (WFF, D), FF ** -0.5, 0.09375, ((0, 32),), (0, 1, 32, 2.75))
    return dict(tokens=tokens, cotangent=cotangent, routed_experts=routed_experts, route_weights=route_weights, gate_matrix=gate_matrix, up_matrix=up_matrix, down_matrix=down_matrix)


def block_sums(hidden, grad_pre_gate, grad_pre_up, gate_cols, up_cols, down_rows):
    blocks = FF // HD
    zero_rows = jnp.zeros((hidden.shape[0], D), jnp.float32)

    def one_block(running, block_pos):
        first_col = (block_pos * HD).astype(jnp.int32)
        hidden_block = lax.dynamic_slice_in_dim(hidden, first_col, HD, 1)
        down_block = lax.dynamic_slice_in_dim(down_rows, first_col, HD, 0)
        gate_block = lax.dynamic_slice_in_dim(gate_cols, first_col, HD, 1)
        up_block = lax.dynamic_slice_in_dim(up_cols, first_col, HD, 1)
        dgate_block = lax.dynamic_slice_in_dim(grad_pre_gate, first_col, HD, 1)
        dup_block = lax.dynamic_slice_in_dim(grad_pre_up, first_col, HD, 1)
        out_part = jnp.dot(hidden_block, down_block, preferred_element_type=jnp.float32)
        out_part = lax.optimization_barrier(out_part.astype(jnp.bfloat16)).astype(jnp.float32)
        back_part = jnp.dot(dgate_block, gate_block.T, preferred_element_type=jnp.float32)
        back_part = back_part + jnp.dot(dup_block, up_block.T, preferred_element_type=jnp.float32)
        back_part = lax.optimization_barrier(back_part.astype(jnp.bfloat16)).astype(jnp.float32)
        return (running[0] + out_part, running[1] + back_part), None

    totals, unused = lax.scan(one_block, (zero_rows, zero_rows), jnp.arange(blocks, dtype=jnp.int32))
    return totals


def reference(tokens, cotangent, routed_experts, route_weights, gate_matrix, up_matrix, down_matrix):
    layer_sum = jnp.zeros((TOKENS, D), jnp.float32)
    back_total = jnp.zeros((TOKENS, D), jnp.float32)
    gate_grads = []
    up_grads = []
    down_grads = []
    for window_pos in range(WIN):
        hits = routed_experts == window_pos
        member = jnp.any(hits, axis=1)
        weight_all = jnp.sum(jnp.where(hits, route_weights, jnp.zeros((), jnp.float32)), axis=1)
        row_order = jnp.argsort(jnp.where(member, 0, 1).astype(jnp.int32), stable=True)[:ROWS].astype(jnp.int32)
        is_valid = member[row_order]
        token_rows = jnp.where(is_valid[:, None], tokens[row_order], jnp.zeros((), tokens.dtype))
        row_weight = jnp.where(is_valid, weight_all[row_order], jnp.zeros((), jnp.float32))
        grad_rows = (row_weight[:, None] * cotangent[row_order].astype(jnp.float32)).astype(jnp.bfloat16)
        gate_cols = gate_matrix[:, window_pos * FF:(window_pos + 1) * FF]
        up_cols = up_matrix[:, window_pos * FF:(window_pos + 1) * FF]
        down_rows = down_matrix[window_pos * FF:(window_pos + 1) * FF, :]
        pre_gate = jnp.dot(token_rows, gate_cols, preferred_element_type=jnp.float32)
        pre_up = jnp.dot(token_rows, up_cols, preferred_element_type=jnp.float32)
        sigmoid_val = jax.nn.sigmoid(pre_gate)
        activated = pre_gate * sigmoid_val
        hidden = (activated * pre_up).astype(jnp.bfloat16)
        grad_hidden = jnp.dot(grad_rows, down_rows.T, preferred_element_type=jnp.float32)
        grad_pre_gate = (grad_hidden * pre_up * (sigmoid_val * (1.0 + pre_gate * (1.0 - sigmoid_val)))).astype(jnp.bfloat16)
        grad_pre_up = (grad_hidden * activated).astype(jnp.bfloat16)
        out_sum, back_sum = block_sums(hidden, grad_pre_gate, grad_pre_up, gate_cols, up_cols, down_rows)
        layer_sum = layer_sum.at[row_order].add(jnp.where(is_valid[:, None], row_weight[:, None] * out_sum, jnp.zeros((), jnp.float32)))
        back_total = back_total.at[row_order].add(jnp.where(is_valid[:, None], back_sum, jnp.zeros((), jnp.float32)))
        gate_grads.append(jnp.dot(token_rows.T, grad_pre_gate, preferred_element_type=jnp.float32).astype(jnp.bfloat16))
        up_grads.append(jnp.dot(token_rows.T, grad_pre_up, preferred_element_type=jnp.float32).astype(jnp.bfloat16))
        down_grads.append(jnp.dot(hidden.T, grad_rows, preferred_element_type=jnp.float32).astype(jnp.bfloat16))
    return (layer_sum.astype(jnp.bfloat16), back_total.astype(jnp.bfloat16), jnp.concatenate(gate_grads, axis=1), jnp.concatenate(up_grads, axis=1), jnp.concatenate(down_grads, axis=0))
```

```python
import jax
import jax.numpy as jnp
from jax import lax
from jax.experimental import pallas as pl
from jax.experimental.pallas import tpu as pltpu
from jax.sharding import PartitionSpec as P

WIN = 2
CAP = 16
VMEM_LIMIT = 56 * 1024 * 1024


def weight_grads(rows, hidden, dgate, dup):
    pieces, _, slots, width = rows.shape
    units = hidden.shape[1]
    per = 2 if units % (32 * pieces) == 0 else 1
    tile = width // per
    high = units // (pieces * per)

    def body(tok_ref, grad_ref, hid_ref, dg_ref, du_ref, og_ref, ou_ref, od_ref):
        tok = tok_ref[0, 0]
        contract = (((0,), (0,)), ((), ()))
        og_ref[...] = lax.dot_general(
            tok, dg_ref[...], contract, preferred_element_type=jnp.float32
        ).astype(jnp.bfloat16)
        ou_ref[...] = lax.dot_general(
            tok, du_ref[...], contract, preferred_element_type=jnp.float32
        ).astype(jnp.bfloat16)
        first = pl.program_id(0) * high
        hid = hid_ref[pl.ds(pl.multiple_of(first, high), high), :]
        for piece in range(pieces):
            od_ref[:, piece * width : (piece + 1) * width] = jnp.dot(
                hid, grad_ref[piece, 0], preferred_element_type=jnp.float32
            ).astype(jnp.bfloat16)

    return pl.pallas_call(
        body,
        grid=(pieces * per,),
        in_specs=[
            pl.BlockSpec((1, 1, slots, tile), lambda i: (i // per, 0, 0, i % per)),
            pl.BlockSpec((pieces, 1, slots, width), lambda i: (0, 1, 0, 0)),
            pl.BlockSpec((units, slots), lambda i: (0, 0)),
            pl.BlockSpec((slots, units), lambda i: (0, 0)),
            pl.BlockSpec((slots, units), lambda i: (0, 0)),
        ],
        out_specs=[
            pl.BlockSpec((tile, units), lambda i: (i, 0)),
            pl.BlockSpec((tile, units), lambda i: (i, 0)),
            pl.BlockSpec((high, pieces * width), lambda i: (i, 0)),
        ],
        out_shape=[
            jax.ShapeDtypeStruct((pieces * width, units), jnp.bfloat16),
            jax.ShapeDtypeStruct((pieces * width, units), jnp.bfloat16),
            jax.ShapeDtypeStruct((units, pieces * width), jnp.bfloat16),
        ],
        compiler_params=pltpu.CompilerParams(vmem_limit_bytes=VMEM_LIMIT),
        cost_estimate=pl.CostEstimate(
            flops=6 * slots * units * pieces * width,
            bytes_accessed=6 * units * pieces * width,
            transcendentals=0,
        ),
    )(rows, rows, hidden.T, dgate, dup)


def local(tokens, cotangent, routed_experts, route_weights, gate, up, down):
    pieces = lax.axis_size("expert")
    groups = lax.axis_size("fsdp")
    per_expert = pieces // WIN
    group_rows, width = tokens.shape
    slots = groups * CAP
    units = gate.shape[1]
    own_ids = lax.dynamic_slice_in_dim(
        routed_experts, lax.axis_index("fsdp") * group_rows, group_rows, 0
    )
    window = jnp.arange(WIN, dtype=jnp.int32)
    hits = own_ids[None] == window[:, None, None]
    member = jnp.any(hits, axis=2)
    weight = jnp.sum(jnp.where(hits, route_weights[None], 0.0), axis=2)
    earlier = jnp.triu(jnp.ones((group_rows, group_rows), jnp.bfloat16), 1)
    place = jnp.dot(member.astype(jnp.bfloat16), earlier, preferred_element_type=jnp.float32)
    chosen = member[:, None, :] & (
        place[:, None, :] == jnp.arange(CAP, dtype=jnp.float32)[None, :, None]
    )
    pick = chosen.astype(jnp.bfloat16).reshape(WIN * CAP, group_rows)
    slot_weight = jnp.sum(jnp.where(chosen, weight[:, None, :], 0.0), axis=2).reshape(-1, 1)
    tok_slots = jnp.dot(pick, tokens, preferred_element_type=jnp.float32).astype(jnp.bfloat16)
    cot_slots = jnp.dot(pick, cotangent, preferred_element_type=jnp.float32)
    grad_slots = (slot_weight * cot_slots).astype(jnp.bfloat16)
    sent = jnp.stack([tok_slots, grad_slots]).reshape(2, WIN, CAP, width).transpose(1, 0, 2, 3)
    sent = jnp.repeat(sent, per_expert, axis=0)
    got = lax.all_to_all(sent, "expert", split_axis=0, concat_axis=0, tiled=True)
    rows = lax.all_gather(got, "fsdp", axis=2, tiled=True)
    tok = rows[:, 0]
    grad = rows[:, 1]
    dims = (pieces, width, units)
    f32 = jnp.float32
    pre_gate = jnp.einsum("etd,edh->th", tok, gate.reshape(dims), preferred_element_type=f32)
    pre_up = jnp.einsum("etd,edh->th", tok, up.reshape(dims), preferred_element_type=f32)
    grad_flat = grad.transpose(1, 0, 2).reshape(slots, pieces * width)
    grad_hidden = jnp.einsum("td,hd->th", grad_flat, down, preferred_element_type=f32)
    sig = jax.nn.sigmoid(pre_gate)
    activated = pre_gate * sig
    hidden = (activated * pre_up).astype(jnp.bfloat16)
    dgate = (grad_hidden * pre_up * (sig * (1.0 + pre_gate * (1.0 - sig)))).astype(jnp.bfloat16)
    dup = (grad_hidden * activated).astype(jnp.bfloat16)
    out_part = jnp.dot(hidden, down, preferred_element_type=f32)
    back_part = jnp.einsum("th,dh->td", dgate, gate, preferred_element_type=f32)
    back_part = back_part + jnp.einsum("th,dh->td", dup, up, preferred_element_type=f32)
    parts = jnp.stack([out_part.astype(jnp.bfloat16), back_part.astype(jnp.bfloat16)])
    parts = parts.reshape(2, slots, pieces, width).transpose(2, 0, 1, 3)
    parts = lax.all_to_all(parts, "expert", split_axis=0, concat_axis=0, tiled=True)
    parts = jnp.sum(
        parts.reshape(WIN, per_expert, 2, groups, CAP, width).astype(f32), axis=1
    ).astype(jnp.bfloat16)
    parts = parts.transpose(2, 0, 1, 3, 4)
    parts = lax.all_to_all(parts, "fsdp", split_axis=0, concat_axis=0, tiled=True)
    total = jnp.sum(parts.astype(f32), axis=0).astype(jnp.bfloat16)
    picked = jnp.einsum(
        "kst,krsd->krtd", pick.reshape(WIN, CAP, group_rows), total, preferred_element_type=f32
    )
    layer = jnp.sum(weight[:, :, None] * picked[:, 0], axis=0).astype(jnp.bfloat16)
    back = jnp.sum(picked[:, 1], axis=0).astype(jnp.bfloat16)
    dgates, dups, ddown = weight_grads(rows, hidden, dgate, dup)
    return layer, back, dgates, dups, ddown


def solution(mesh):
    columns = P(None, ("expert", "fsdp"))
    lines = P(("expert", "fsdp"), None)
    split = P("fsdp", "expert")
    return jax.shard_map(
        local,
        mesh=mesh,
        in_specs=(split, split, P(), P("fsdp", None), columns, columns, lines),
        out_specs=(split, split, columns, columns, lines),
        check_vma=False,
    )
```

```python
import jax
import jax.numpy as jnp
from jax import lax
from jax.experimental import pallas as pl
from jax.experimental.pallas import tpu as pltpu
from jax.sharding import PartitionSpec as P

WIN = 2
CAP = 16
VMEM_LIMIT = 56 * 1024 * 1024


def weight_grads(rows, hidden, dgate, dup):
    pieces, _, slots, width = rows.shape
    units = hidden.shape[1]
    per = 2 if units % (32 * pieces) == 0 else 1
    tile = width // per
    high = units // (pieces * per)

    def body(tok_ref, grad_ref, hid_ref, dg_ref, du_ref, og_ref, ou_ref, od_ref):
        tok = tok_ref[0, 0]
        contract = (((0,), (0,)), ((), ()))
        og_ref[...] = lax.dot_general(
            tok, dg_ref[...], contract, preferred_element_type=jnp.float32
        ).astype(jnp.bfloat16)
        ou_ref[...] = lax.dot_general(
            tok, du_ref[...], contract, preferred_element_type=jnp.float32
        ).astype(jnp.bfloat16)
        first = pl.program_id(0) * high
        hid = hid_ref[pl.ds(pl.multiple_of(first, high), high), :]
        for piece in range(pieces):
            od_ref[:, piece * width : (piece + 1) * width] = jnp.dot(
                hid, grad_ref[piece, 0], preferred_element_type=jnp.float32
            ).astype(jnp.bfloat16)

    return pl.pallas_call(
        body,
        grid=(pieces * per,),
        in_specs=[
            pl.BlockSpec((1, 1, slots, tile), lambda i: (i // per, 0, 0, i % per)),
            pl.BlockSpec((pieces, 1, slots, width), lambda i: (0, 1, 0, 0)),
            pl.BlockSpec((units, slots), lambda i: (0, 0)),
            pl.BlockSpec((slots, units), lambda i: (0, 0)),
            pl.BlockSpec((slots, units), lambda i: (0, 0)),
        ],
        out_specs=[
            pl.BlockSpec((tile, units), lambda i: (i, 0)),
            pl.BlockSpec((tile, units), lambda i: (i, 0)),
            pl.BlockSpec((high, pieces * width), lambda i: (i, 0)),
        ],
        out_shape=[
            jax.ShapeDtypeStruct((pieces * width, units), jnp.bfloat16),
            jax.ShapeDtypeStruct((pieces * width, units), jnp.bfloat16),
            jax.ShapeDtypeStruct((units, pieces * width), jnp.bfloat16),
        ],
        compiler_params=pltpu.CompilerParams(vmem_limit_bytes=VMEM_LIMIT),
        cost_estimate=pl.CostEstimate(
            flops=6 * slots * units * pieces * width,
            bytes_accessed=6 * units * pieces * width,
            transcendentals=0,
        ),
    )(rows, rows, hidden.T, dgate, dup)


def exchange_and_products(pick, slot_weight, weight, tokens, cotangent, gate, up, down):
    pieces = lax.axis_size("expert")
    groups = lax.axis_size("fsdp")
    per_expert = pieces // WIN
    depth = groups // 2
    group_rows, width = tokens.shape
    slots = groups * CAP
    half = slots // 2
    units = gate.shape[1]
    bf16, f32 = jnp.bfloat16, jnp.float32
    unit_tile = min(256, units)
    col_tile = 512 if width % 512 == 0 else 256
    n_copies = (depth - 1) + depth * (pieces - 1) + depth * pieces + pieces + (pieces - 1) + (depth - 1)
    rows_t = (((0,), (0,)), ((), ()))
    cols_t = (((1,), (1,)), ((), ()))

    def body(
        pick_ref, sw_ref, w_ref, tok_ref, cot_ref, gate_hbm, up_hbm, down_hbm,
        layer_ref, back_ref, hid_ref, dg_ref, du_ref, rows_out,
        gate_v, up_v, down_v, held, rows, parts, paired, spread, summed, landed,
        load_sem, send_sem, recv_sem,
    ):
        e = lax.axis_index("expert")
        f = lax.axis_index("fsdp")
        z = f // 2
        c = lax.rem(f, 2)
        own = e // per_expert
        counter = [0]
        started = []

        def send(src, dst, to_e, to_f):
            at = counter[0]
            counter[0] += 1
            copy = pltpu.make_async_remote_copy(
                src_ref=src,
                dst_ref=dst,
                send_sem=send_sem.at[at],
                recv_sem=recv_sem.at[at],
                device_id={"expert": to_e, "fsdp": to_f},
                device_id_type=pl.DeviceIdType.MESH,
            )
            copy.start()
            started.append(copy)
            return copy

        def other_e(i):
            return lax.rem(e + i, pieces)

        def other_z(j):
            return lax.rem(z + j, depth)

        barrier = pltpu.get_barrier_semaphore()
        partners = [(e, other_z(j) * 2 + c) for j in range(1, depth)]
        partners += [(other_e(i), f) for i in range(1, pieces)]
        partners += [(e, z * 2 + 1 - c)]
        for to_e, to_f in partners:
            pl.semaphore_signal(
                barrier,
                inc=1,
                device_id={"expert": to_e, "fsdp": to_f},
                device_id_type=pl.DeviceIdType.MESH,
            )

        loads = []
        for which, (src, dst) in enumerate(((gate_hbm, gate_v), (up_hbm, up_v), (down_hbm, down_v))):
            step = src.shape[0] // pieces
            for piece in range(pieces):
                span = pl.ds(piece * step, step)
                load = pltpu.make_async_copy(
                    src.at[span], dst.at[span], load_sem.at[which * pieces + piece]
                )
                load.start()
                loads.append(load)

        tok_slots = jnp.dot(pick_ref[...], tok_ref[...], preferred_element_type=f32).astype(bf16)
        cot_slots = jnp.dot(pick_ref[...], cot_ref[...], preferred_element_type=f32)
        grad_slots = (sw_ref[...] * cot_slots).astype(bf16)
        for k in range(WIN):
            held[z, k, 0] = tok_slots[k * CAP : (k + 1) * CAP]
            held[z, k, 1] = grad_slots[k * CAP : (k + 1) * CAP]
        pl.semaphore_wait(barrier, len(partners))

        along = [
            send(held.at[z], held.at[z], e, other_z(j) * 2 + c) for j in range(1, depth)
        ]
        across = {}
        beside = []

        def place(zs):
            return pl.ds(pl.multiple_of((c * depth + zs) * CAP, CAP), CAP)

        def pass_on(j):
            zs = lax.rem(z - j + depth, depth)
            for i in range(pieces):
                if i > 0:
                    across[j, i].wait_recv()
                came = lax.rem(e - i + pieces, pieces)
                spot = rows.at[came, :, place(zs), :]
                beside.append(send(spot, spot, e, z * 2 + 1 - c))

        for j in range(depth):
            zs = lax.rem(z - j + depth, depth)
            if j > 0:
                along[j - 1].wait_recv()
            for i in range(1, pieces):
                to_e = other_e(i)
                across[j, i] = send(
                    held.at[zs, to_e // per_expert], rows.at[e, :, place(zs), :], to_e, f
                )
            rows[e, :, place(zs), :] = held[zs, own]
            if j > 0:
                pass_on(j - 1)
        pass_on(depth - 1)
        for copy in beside:
            copy.wait_recv()
        keep = pltpu.make_async_copy(rows, rows_out, load_sem.at[3 * pieces])
        keep.start()
        for load in loads:
            load.wait()

        def forward(t, carry):
            span = pl.ds(pl.multiple_of(t * unit_tile, unit_tile), unit_tile)
            pre_gate = pre_up = grad_hidden = 0.0
            for piece in range(pieces):
                cols = slice(piece * width, (piece + 1) * width)
                tok = rows[piece, 0]
                pre_gate += jnp.dot(tok, gate_v[cols, span], preferred_element_type=f32)
                pre_up += jnp.dot(tok, up_v[cols, span], preferred_element_type=f32)
                grad_hidden += lax.dot_general(
                    rows[piece, 1], down_v[span, cols], cols_t, preferred_element_type=f32
                )
            sig = jax.nn.sigmoid(pre_gate)
            activated = pre_gate * sig
            hid_ref[:, span] = (activated * pre_up).astype(bf16)
            dg_ref[:, span] = (
                grad_hidden * pre_up * (sig * (1.0 + pre_gate * (1.0 - sig)))
            ).astype(bf16)
            du_ref[:, span] = (grad_hidden * activated).astype(bf16)
            return carry

        lax.fori_loop(0, units // unit_tile, forward, 0)

        mine = pl.ds(pl.multiple_of(c * half, CAP), half)
        theirs = pl.ds(pl.multiple_of((1 - c) * half, CAP), half)
        pairs = []
        spreads = []

        def finish(i):
            to_e = other_e(i + 1)
            pairs[i].wait_recv()
            both = parts[to_e, :, mine, :].astype(f32) + paired[to_e].astype(f32)
            if i < pieces - 1:
                parts[to_e, :, mine, :] = both.astype(bf16)
                spreads.append(send(parts.at[to_e, :, mine, :], spread.at[e], to_e, f))
            else:
                spread[e] = both.astype(bf16)

        for i in range(pieces):
            to_e = other_e(i + 1)

            def backward(t, carry):
                spot = pl.ds(pl.multiple_of(t * col_tile, col_tile), col_tile)
                cols = pl.ds(pl.multiple_of(to_e * width + t * col_tile, 128), col_tile)
                parts[to_e, 0, :, spot] = jnp.dot(
                    hid_ref[...], down_v[:, cols], preferred_element_type=f32
                ).astype(bf16)
                back = lax.dot_general(
                    dg_ref[...], gate_v[cols, :], cols_t, preferred_element_type=f32
                )
                back += lax.dot_general(
                    du_ref[...], up_v[cols, :], cols_t, preferred_element_type=f32
                )
                parts[to_e, 1, :, spot] = back.astype(bf16)
                return carry

            lax.fori_loop(0, width // col_tile, backward, 0)
            pairs.append(
                send(parts.at[to_e, :, theirs, :], paired.at[to_e], e, z * 2 + 1 - c)
            )
            if i > 0:
                finish(i - 1)
        finish(pieces - 1)
        for copy in spreads:
            copy.wait_recv()

        returns = []
        for j in list(range(1, depth)) + [0]:
            to_z = other_z(j)
            span = pl.ds(pl.multiple_of(to_z * CAP, CAP), CAP)
            for k in range(WIN):
                total = 0.0
                for piece in range(k * per_expert, (k + 1) * per_expert):
                    total += spread[piece, :, span, :].astype(f32)
                if j > 0:
                    summed[j, k] = total.astype(bf16)
                else:
                    landed[z, k] = total.astype(bf16)
            if j > 0:
                returns.append(send(summed.at[j], landed.at[z], e, to_z * 2 + c))
        for copy in returns:
            copy.wait_recv()

        layer = jnp.zeros((group_rows, width), f32)
        back = jnp.zeros((group_rows, width), f32)
        for k in range(WIN):
            total = 0.0
            for zs in range(depth):
                total += landed[zs, k].astype(f32)
            total = total.astype(bf16)
            choice = pick_ref[k * CAP : (k + 1) * CAP, :]
            layer += w_ref[:, k : k + 1] * lax.dot_general(
                choice, total[0], rows_t, preferred_element_type=f32
            )
            back += lax.dot_general(choice, total[1], rows_t, preferred_element_type=f32)
        layer_ref[...] = layer.astype(bf16)
        back_ref[...] = back.astype(bf16)
        for copy in started:
            copy.wait_send()
        keep.wait()

    vmem = pl.BlockSpec(memory_space=pltpu.VMEM)
    anywhere = pl.BlockSpec(memory_space=pl.ANY)
    shape = jax.ShapeDtypeStruct
    return pl.pallas_call(
        body,
        in_specs=[vmem] * 5 + [anywhere] * 3,
        out_specs=[vmem] * 5 + [anywhere],
        out_shape=[
            shape((group_rows, width), bf16),
            shape((group_rows, width), bf16),
            shape((slots, units), bf16),
            shape((slots, units), bf16),
            shape((slots, units), bf16),
            shape((pieces, 2, slots, width), bf16),
        ],
        scratch_shapes=[
            pltpu.VMEM(gate.shape, bf16),
            pltpu.VMEM(up.shape, bf16),
            pltpu.VMEM(down.shape, bf16),
            pltpu.VMEM((depth, WIN, 2, CAP, width), bf16),
            pltpu.VMEM((pieces, 2, slots, width), bf16),
            pltpu.VMEM((pieces, 2, slots, width), bf16),
            pltpu.VMEM((pieces, 2, half, width), bf16),
            pltpu.VMEM((pieces, 2, half, width), bf16),
            pltpu.VMEM((depth, WIN, 2, CAP, width), bf16),
            pltpu.VMEM((depth, WIN, 2, CAP, width), bf16),
            pltpu.SemaphoreType.DMA((3 * pieces + 1,)),
            pltpu.SemaphoreType.DMA((n_copies,)),
            pltpu.SemaphoreType.DMA((n_copies,)),
        ],
        compiler_params=pltpu.CompilerParams(
            collective_id=0, has_side_effects=True, vmem_limit_bytes=62 * 1024 * 1024
        ),
        cost_estimate=pl.CostEstimate(
            flops=12 * slots * units * pieces * width,
            bytes_accessed=6 * units * pieces * width,
            transcendentals=slots * units,
        ),
    )(pick, slot_weight, weight, tokens, cotangent, gate, up, down)


def local(tokens, cotangent, routed_experts, route_weights, gate, up, down):
    group_rows = tokens.shape[0]
    own_ids = lax.dynamic_slice_in_dim(
        routed_experts, lax.axis_index("fsdp") * group_rows, group_rows, 0
    )
    window = jnp.arange(WIN, dtype=jnp.int32)
    hits = own_ids[None] == window[:, None, None]
    member = jnp.any(hits, axis=2)
    weight = jnp.sum(jnp.where(hits, route_weights[None], 0.0), axis=2)
    earlier = jnp.triu(jnp.ones((group_rows, group_rows), jnp.bfloat16), 1)
    place = jnp.dot(member.astype(jnp.bfloat16), earlier, preferred_element_type=jnp.float32)
    chosen = member[:, None, :] & (
        place[:, None, :] == jnp.arange(CAP, dtype=jnp.float32)[None, :, None]
    )
    pick = chosen.astype(jnp.bfloat16).reshape(WIN * CAP, group_rows)
    slot_weight = jnp.sum(jnp.where(chosen, weight[:, None, :], 0.0), axis=2).reshape(-1, 1)
    layer, back, hidden, dgate, dup, rows = exchange_and_products(
        pick, slot_weight, weight.T, tokens, cotangent, gate, up, down
    )
    dgates, dups, ddown = weight_grads(rows, hidden, dgate, dup)
    return layer, back, dgates, dups, ddown


def solution(mesh):
    columns = P(None, ("expert", "fsdp"))
    lines = P(("expert", "fsdp"), None)
    split = P("fsdp", "expert")
    return jax.shard_map(
        local,
        mesh=mesh,
        in_specs=(split, split, P(), P("fsdp", None), columns, columns, lines),
        out_specs=(split, split, columns, columns, lines),
        check_vma=False,
    )
```

```python
import jax
import jax.numpy as jnp
from jax import lax
from jax.experimental import pallas as pl
from jax.experimental.pallas import tpu as pltpu
from jax.sharding import PartitionSpec as P

WIN = 2
CAP = 16
VMEM_LIMIT = 56 * 1024 * 1024


def weight_grads(rows, hidden_t, dgate, dup):
    pieces, _, slots, width = rows.shape
    units = dgate.shape[1]
    per = 4 if units % (64 * pieces) == 0 and width % 512 == 0 else 1
    tile = width // per
    high = units // (pieces * per)

    def body(tok_ref, grad_ref, hid_ref, dg_ref, du_ref, og_ref, ou_ref, od_ref):
        tok = tok_ref[0, 0]
        contract = (((0,), (0,)), ((), ()))
        og_ref[...] = lax.dot_general(
            tok, dg_ref[...], contract, preferred_element_type=jnp.float32
        ).astype(jnp.bfloat16)
        ou_ref[...] = lax.dot_general(
            tok, du_ref[...], contract, preferred_element_type=jnp.float32
        ).astype(jnp.bfloat16)
        first = pl.program_id(0) * high
        hid = hid_ref[pl.ds(pl.multiple_of(first, high), high), :]
        for piece in range(pieces):
            od_ref[:, piece * width : (piece + 1) * width] = jnp.dot(
                hid, grad_ref[piece, 0], preferred_element_type=jnp.float32
            ).astype(jnp.bfloat16)

    return pl.pallas_call(
        body,
        grid=(pieces * per,),
        in_specs=[
            pl.BlockSpec((1, 1, slots, tile), lambda i: (i // per, 0, 0, i % per)),
            pl.BlockSpec((pieces, 1, slots, width), lambda i: (0, 1, 0, 0)),
            pl.BlockSpec((units, slots), lambda i: (0, 0)),
            pl.BlockSpec((slots, units), lambda i: (0, 0)),
            pl.BlockSpec((slots, units), lambda i: (0, 0)),
        ],
        out_specs=[
            pl.BlockSpec((tile, units), lambda i: (i, 0)),
            pl.BlockSpec((tile, units), lambda i: (i, 0)),
            pl.BlockSpec((high, pieces * width), lambda i: (i, 0)),
        ],
        out_shape=[
            jax.ShapeDtypeStruct((pieces * width, units), jnp.bfloat16),
            jax.ShapeDtypeStruct((pieces * width, units), jnp.bfloat16),
            jax.ShapeDtypeStruct((units, pieces * width), jnp.bfloat16),
        ],
        compiler_params=pltpu.CompilerParams(vmem_limit_bytes=VMEM_LIMIT),
        cost_estimate=pl.CostEstimate(
            flops=6 * slots * units * pieces * width,
            bytes_accessed=6 * units * pieces * width,
            transcendentals=0,
        ),
    )(rows, rows, hidden_t, dgate, dup)


def exchange_and_products(pick, ids, weights, tokens, cotangent, gate, up, down):
    pieces = lax.axis_size("expert")
    groups = lax.axis_size("fsdp")
    per_expert = pieces // WIN
    depth = groups // 2
    group_rows, width = tokens.shape
    slots = groups * CAP
    half = slots // 2
    units = gate.shape[1]
    bf16, f32 = jnp.bfloat16, jnp.float32
    unit_tile = min(256, units)
    col_tile = 512 if width % 512 == 0 else 256
    n_copies = (depth - 1) + depth * (pieces - 1) + depth * pieces + pieces + depth * (pieces - 1) + (depth - 1)
    rows_t = (((0,), (0,)), ((), ()))
    cols_t = (((1,), (1,)), ((), ()))

    def body(
        pick_ref, ids_ref, w_ref, tok_ref, cot_ref, gate_hbm, up_hbm, down_hbm,
        layer_ref, back_ref, hidt_ref, dg_ref, du_ref, rows_out,
        gate_v, up_v, down_v, held, rows, parts, paired, spread, summed, landed, hid_ref, sums,
        load_sem, send_sem, recv_sem,
    ):
        e = lax.axis_index("expert")
        f = lax.axis_index("fsdp")
        z = f // 2
        c = lax.rem(f, 2)
        own = e // per_expert
        counter = [0]
        started = []

        def send(src, dst, to_e, to_f):
            at = counter[0]
            counter[0] += 1
            copy = pltpu.make_async_remote_copy(
                src_ref=src,
                dst_ref=dst,
                send_sem=send_sem.at[at],
                recv_sem=recv_sem.at[at],
                device_id={"expert": to_e, "fsdp": to_f},
                device_id_type=pl.DeviceIdType.MESH,
            )
            copy.start()
            started.append(copy)
            return copy

        def other_e(i):
            return lax.rem(e + i, pieces)

        def other_z(j):
            return lax.rem(z + j, depth)

        barrier = pltpu.get_barrier_semaphore()
        partners = [(e, other_z(j) * 2 + c) for j in range(1, depth)]
        partners += [(other_e(i), f) for i in range(1, pieces)]
        partners += [(e, z * 2 + 1 - c)]
        for to_e, to_f in partners:
            pl.semaphore_signal(
                barrier,
                inc=1,
                device_id={"expert": to_e, "fsdp": to_f},
                device_id_type=pl.DeviceIdType.MESH,
            )

        loads = []
        for which, (src, dst) in enumerate(((gate_hbm, gate_v), (up_hbm, up_v), (down_hbm, down_v))):
            step = src.shape[0] // pieces
            for piece in range(pieces):
                span = pl.ds(piece * step, step)
                load = pltpu.make_async_copy(
                    src.at[span], dst.at[span], load_sem.at[which * pieces + piece]
                )
                load.start()
                loads.append(load)

        tok_slots = jnp.dot(pick_ref[...], tok_ref[...], preferred_element_type=f32).astype(bf16)
        cot = cot_ref[...].astype(f32)
        row_weight = [
            jnp.sum(jnp.where(ids_ref[...] == k, w_ref[...], 0.0), axis=1, keepdims=True)
            for k in range(WIN)
        ]
        for k in range(WIN):
            held[z, k, 0] = tok_slots[k * CAP : (k + 1) * CAP]
            held[z, k, 1] = jnp.dot(
                pick_ref[k * CAP : (k + 1) * CAP, :],
                (row_weight[k] * cot).astype(bf16),
                preferred_element_type=f32,
            ).astype(bf16)
        pl.semaphore_wait(barrier, len(partners))

        along = [
            send(held.at[z], held.at[z], e, other_z(j) * 2 + c) for j in range(1, depth)
        ]
        across = {}
        beside = []

        own_beside = []

        def came_from(i):
            return lax.rem(e - i + pieces, pieces)

        def products(piece, span):
            lines = pl.ds(pl.multiple_of(piece * width, 128), width)
            tok = rows[piece, 0]
            return (
                jnp.dot(tok, gate_v[lines, span], preferred_element_type=f32),
                jnp.dot(tok, up_v[lines, span], preferred_element_type=f32),
                lax.dot_general(
                    rows[piece, 1], down_v[span, lines], cols_t, preferred_element_type=f32
                ),
            )

        def first(t, carry):
            span = pl.ds(pl.multiple_of(t * unit_tile, unit_tile), unit_tile)
            for at, term in enumerate(products(e, span)):
                sums[at, :, span] = term
            return carry

        def place(zs):
            return pl.ds(pl.multiple_of((c * depth + zs) * CAP, CAP), CAP)

        def pass_on(j):
            zs = lax.rem(z - j + depth, depth)
            for i in range(1, pieces):
                across[j, i].wait_recv()
                spot = rows.at[came_from(i), :, place(zs), :]
                beside.append(send(spot, spot, e, z * 2 + 1 - c))

        for j in range(depth):
            zs = lax.rem(z - j + depth, depth)
            if j > 0:
                along[j - 1].wait_recv()
            for i in range(1, pieces):
                to_e = other_e(i)
                across[j, i] = send(
                    held.at[zs, to_e // per_expert], rows.at[e, :, place(zs), :], to_e, f
                )
            rows[e, :, place(zs), :] = held[zs, own]
            spot = rows.at[e, :, place(zs), :]
            own_beside.append(send(spot, spot, e, z * 2 + 1 - c))
            if j > 0:
                pass_on(j - 1)
        for load in loads:
            load.wait()
        for copy in own_beside:
            copy.wait_recv()
        lax.fori_loop(0, units // unit_tile, first, 0)
        pass_on(depth - 1)
        for copy in beside:
            copy.wait_recv()
        keep = pltpu.make_async_copy(rows, rows_out, load_sem.at[3 * pieces])
        keep.start()

        def forward(t, carry):
            span = pl.ds(pl.multiple_of(t * unit_tile, unit_tile), unit_tile)
            pre_gate, pre_up, grad_hidden = (sums[at, :, span] for at in range(3))
            for i in range(1, pieces):
                more = products(came_from(i), span)
                pre_gate += more[0]
                pre_up += more[1]
                grad_hidden += more[2]
            sig = jax.nn.sigmoid(pre_gate)
            activated = pre_gate * sig
            hid = activated * pre_up
            hid_ref[:, span] = hid.astype(bf16)
            hidt_ref[span, :] = hid.T.astype(bf16)
            dg_ref[:, span] = (
                grad_hidden * pre_up * (sig * (1.0 + pre_gate * (1.0 - sig)))
            ).astype(bf16)
            du_ref[:, span] = (grad_hidden * activated).astype(bf16)
            return carry

        lax.fori_loop(0, units // unit_tile, forward, 0)

        mine = pl.ds(pl.multiple_of(c * half, CAP), half)
        theirs = pl.ds(pl.multiple_of((1 - c) * half, CAP), half)
        pairs = []
        spreads = {}
        early = list(range(1, depth // 2 + 1))
        late = [j for j in range(depth) if j not in early and j > 0] + [0]

        def spread_out(i, j):
            to_e = other_e(i + 1)
            to_z = other_z(j)
            spreads[i, j] = send(
                parts.at[to_e, :, place(to_z), :],
                spread.at[e, :, pl.ds(pl.multiple_of(to_z * CAP, CAP), CAP), :],
                to_e,
                f,
            )

        def finish(i):
            to_e = other_e(i + 1)
            pairs[i].wait_recv()
            both = parts[to_e, :, mine, :].astype(f32) + paired[to_e].astype(f32)
            if i < pieces - 1:
                parts[to_e, :, mine, :] = both.astype(bf16)
                for j in early:
                    spread_out(i, j)
            else:
                spread[e] = both.astype(bf16)

        for i in range(pieces):
            to_e = other_e(i + 1)

            def backward(t, carry):
                spot = pl.ds(pl.multiple_of(t * col_tile, col_tile), col_tile)
                cols = pl.ds(pl.multiple_of(to_e * width + t * col_tile, 128), col_tile)
                parts[to_e, 0, :, spot] = jnp.dot(
                    hid_ref[...], down_v[:, cols], preferred_element_type=f32
                ).astype(bf16)
                back = lax.dot_general(
                    dg_ref[...], gate_v[cols, :], cols_t, preferred_element_type=f32
                )
                back += lax.dot_general(
                    du_ref[...], up_v[cols, :], cols_t, preferred_element_type=f32
                )
                parts[to_e, 1, :, spot] = back.astype(bf16)
                return carry

            lax.fori_loop(0, width // col_tile, backward, 0)
            pairs.append(
                send(parts.at[to_e, :, theirs, :], paired.at[to_e], e, z * 2 + 1 - c)
            )
            if i > 0:
                finish(i - 1)
        finish(pieces - 1)
        for j in late:
            for i in range(pieces - 1):
                spread_out(i, j)

        returns = []
        for j in early + late:
            for i in range(pieces - 1):
                spreads[i, j].wait_recv()
            to_z = other_z(j)
            span = pl.ds(pl.multiple_of(to_z * CAP, CAP), CAP)
            for k in range(WIN):
                total = 0.0
                for piece in range(k * per_expert, (k + 1) * per_expert):
                    total += spread[piece, :, span, :].astype(f32)
                if j > 0:
                    summed[j, k] = total.astype(bf16)
                else:
                    landed[z, k] = total.astype(bf16)
            if j > 0:
                returns.append(send(summed.at[j], landed.at[z], e, to_z * 2 + c))
        for copy in returns:
            copy.wait_recv()

        layer = jnp.zeros((group_rows, width), f32)
        back = jnp.zeros((group_rows, width), f32)
        for k in range(WIN):
            total = 0.0
            for zs in range(depth):
                total += landed[zs, k].astype(f32)
            total = total.astype(bf16)
            choice = pick_ref[k * CAP : (k + 1) * CAP, :]
            layer += row_weight[k] * lax.dot_general(
                choice, total[0], rows_t, preferred_element_type=f32
            )
            back += lax.dot_general(choice, total[1], rows_t, preferred_element_type=f32)
        layer_ref[...] = layer.astype(bf16)
        back_ref[...] = back.astype(bf16)
        for copy in started:
            copy.wait_send()
        keep.wait()

    vmem = pl.BlockSpec(memory_space=pltpu.VMEM)
    anywhere = pl.BlockSpec(memory_space=pl.ANY)
    shape = jax.ShapeDtypeStruct
    return pl.pallas_call(
        body,
        in_specs=[vmem] * 5 + [anywhere] * 3,
        out_specs=[vmem] * 5 + [anywhere],
        out_shape=[
            shape((group_rows, width), bf16),
            shape((group_rows, width), bf16),
            shape((units, slots), bf16),
            shape((slots, units), bf16),
            shape((slots, units), bf16),
            shape((pieces, 2, slots, width), bf16),
        ],
        scratch_shapes=[
            pltpu.VMEM(gate.shape, bf16),
            pltpu.VMEM(up.shape, bf16),
            pltpu.VMEM(down.shape, bf16),
            pltpu.VMEM((depth, WIN, 2, CAP, width), bf16),
            pltpu.VMEM((pieces, 2, slots, width), bf16),
            pltpu.VMEM((pieces, 2, slots, width), bf16),
            pltpu.VMEM((pieces, 2, half, width), bf16),
            pltpu.VMEM((pieces, 2, half, width), bf16),
            pltpu.VMEM((depth, WIN, 2, CAP, width), bf16),
            pltpu.VMEM((depth, WIN, 2, CAP, width), bf16),
            pltpu.VMEM((slots, units), bf16),
            pltpu.VMEM((3, slots, units), f32),
            pltpu.SemaphoreType.DMA((3 * pieces + 1,)),
            pltpu.SemaphoreType.DMA((n_copies,)),
            pltpu.SemaphoreType.DMA((n_copies,)),
        ],
        compiler_params=pltpu.CompilerParams(
            collective_id=0, has_side_effects=True, vmem_limit_bytes=62 * 1024 * 1024
        ),
        cost_estimate=pl.CostEstimate(
            flops=12 * slots * units * pieces * width,
            bytes_accessed=6 * units * pieces * width,
            transcendentals=slots * units,
        ),
    )(pick, ids, weights, tokens, cotangent, gate, up, down)


def local(tokens, cotangent, routed_experts, route_weights, gate, up, down):
    group_rows = tokens.shape[0]
    own_ids = lax.dynamic_slice_in_dim(
        routed_experts, lax.axis_index("fsdp") * group_rows, group_rows, 0
    )
    window = jnp.arange(WIN, dtype=jnp.int32)
    hits = own_ids[None] == window[:, None, None]
    member = jnp.any(hits, axis=2)
    earlier = jnp.triu(jnp.ones((group_rows, group_rows), jnp.bfloat16), 1)
    place = jnp.dot(member.astype(jnp.bfloat16), earlier, preferred_element_type=jnp.float32)
    chosen = member[:, None, :] & (
        place[:, None, :] == jnp.arange(CAP, dtype=jnp.float32)[None, :, None]
    )
    pick = chosen.astype(jnp.bfloat16).reshape(WIN * CAP, group_rows)
    layer, back, hidden_t, dgate, dup, rows = exchange_and_products(
        pick, own_ids, route_weights, tokens, cotangent, gate, up, down
    )
    dgates, dups, ddown = weight_grads(rows, hidden_t, dgate, dup)
    return layer, back, dgates, dups, ddown


def solution(mesh):
    columns = P(None, ("expert", "fsdp"))
    lines = P(("expert", "fsdp"), None)
    split = P("fsdp", "expert")
    return jax.shard_map(
        local,
        mesh=mesh,
        in_specs=(split, split, P(), P("fsdp", None), columns, columns, lines),
        out_specs=(split, split, columns, columns, lines),
        check_vma=False,
    )
```

```python
import jax
import jax.numpy as jnp
from jax import lax
from jax.experimental import pallas as pl
from jax.experimental.pallas import tpu as pltpu
from jax.sharding import PartitionSpec as P

WIN = 2
CAP = 16
VMEM_LIMIT = 56 * 1024 * 1024


def weight_grads(rows, hidden_t, dgate, dup):
    pieces, _, slots, width = rows.shape
    units = dgate.shape[1]
    per = 2 if width % 256 == 0 else 1
    tile = width // per

    def body(tok_ref, grad_ref, hid_ref, dg_ref, du_ref, og_ref, ou_ref, od_ref):
        tok = tok_ref[0, 0]
        contract = (((0,), (0,)), ((), ()))
        og_ref[...] = lax.dot_general(
            tok, dg_ref[...], contract, preferred_element_type=jnp.float32
        ).astype(jnp.bfloat16)
        ou_ref[...] = lax.dot_general(
            tok, du_ref[...], contract, preferred_element_type=jnp.float32
        ).astype(jnp.bfloat16)
        od_ref[...] = jnp.dot(
            hid_ref[...], grad_ref[0, 0], preferred_element_type=jnp.float32
        ).astype(jnp.bfloat16)

    return pl.pallas_call(
        body,
        grid=(pieces * per,),
        in_specs=[
            pl.BlockSpec((1, 1, slots, tile), lambda i: (i // per, 0, 0, i % per)),
            pl.BlockSpec((1, 1, slots, tile), lambda i: (i // per, 1, 0, i % per)),
            pl.BlockSpec((units, slots), lambda i: (0, 0)),
            pl.BlockSpec((slots, units), lambda i: (0, 0)),
            pl.BlockSpec((slots, units), lambda i: (0, 0)),
        ],
        out_specs=[
            pl.BlockSpec((tile, units), lambda i: (i, 0)),
            pl.BlockSpec((tile, units), lambda i: (i, 0)),
            pl.BlockSpec((units, tile), lambda i: (0, i)),
        ],
        out_shape=[
            jax.ShapeDtypeStruct((pieces * width, units), jnp.bfloat16),
            jax.ShapeDtypeStruct((pieces * width, units), jnp.bfloat16),
            jax.ShapeDtypeStruct((units, pieces * width), jnp.bfloat16),
        ],
        compiler_params=pltpu.CompilerParams(vmem_limit_bytes=VMEM_LIMIT),
        cost_estimate=pl.CostEstimate(
            flops=6 * slots * units * pieces * width,
            bytes_accessed=6 * units * pieces * width,
            transcendentals=0,
        ),
    )(rows, rows, hidden_t, dgate, dup)


def exchange_and_products(pick, ids, weights, tokens, cotangent, gate, up, down):
    pieces = lax.axis_size("expert")
    groups = lax.axis_size("fsdp")
    per_expert = pieces // WIN
    depth = groups // 2
    group_rows, width = tokens.shape
    slots = groups * CAP
    half = slots // 2
    units = gate.shape[1]
    bf16, f32 = jnp.bfloat16, jnp.float32
    unit_tile = min(256, units)
    col_tile = 512 if width % 512 == 0 else 256
    n_copies = (depth - 1) + depth * (pieces - 1) + depth * pieces + pieces + depth * (pieces - 1) + (depth - 1)
    rows_t = (((0,), (0,)), ((), ()))
    cols_t = (((1,), (1,)), ((), ()))

    def body(
        pick_ref, ids_ref, w_ref, tok_ref, cot_ref, gate_hbm, up_hbm, down_hbm,
        layer_ref, back_ref, hidt_ref, dg_ref, du_ref, rows_out,
        gate_v, up_v, down_v, held, rows, parts, paired, spread, summed, landed, hid_ref, sums,
        load_sem, send_sem, recv_sem,
    ):
        e = lax.axis_index("expert")
        f = lax.axis_index("fsdp")
        z = f // 2
        c = lax.rem(f, 2)
        own = e // per_expert
        counter = [0]
        started = []

        def send(src, dst, to_e, to_f):
            at = counter[0]
            counter[0] += 1
            copy = pltpu.make_async_remote_copy(
                src_ref=src,
                dst_ref=dst,
                send_sem=send_sem.at[at],
                recv_sem=recv_sem.at[at],
                device_id={"expert": to_e, "fsdp": to_f},
                device_id_type=pl.DeviceIdType.MESH,
            )
            copy.start()
            started.append(copy)
            return copy

        def other_e(i):
            return lax.rem(e + i, pieces)

        def other_z(j):
            return lax.rem(z + j, depth)

        barrier = pltpu.get_barrier_semaphore()
        partners = [(e, other_z(j) * 2 + c) for j in range(1, depth)]
        partners += [(other_e(i), f) for i in range(1, pieces)]
        partners += [(e, z * 2 + 1 - c)]
        for to_e, to_f in partners:
            pl.semaphore_signal(
                barrier,
                inc=1,
                device_id={"expert": to_e, "fsdp": to_f},
                device_id_type=pl.DeviceIdType.MESH,
            )

        loads = []
        for which, (src, dst) in enumerate(((gate_hbm, gate_v), (up_hbm, up_v), (down_hbm, down_v))):
            step = src.shape[0] // pieces
            for piece in range(pieces):
                span = pl.ds(piece * step, step)
                load = pltpu.make_async_copy(
                    src.at[span], dst.at[span], load_sem.at[which * pieces + piece]
                )
                load.start()
                loads.append(load)

        tok_slots = jnp.dot(pick_ref[...], tok_ref[...], preferred_element_type=f32).astype(bf16)
        cot = cot_ref[...].astype(f32)
        row_weight = [
            jnp.sum(jnp.where(ids_ref[...] == k, w_ref[...], 0.0), axis=1, keepdims=True)
            for k in range(WIN)
        ]
        for k in range(WIN):
            held[z, k, 0] = tok_slots[k * CAP : (k + 1) * CAP]
            held[z, k, 1] = jnp.dot(
                pick_ref[k * CAP : (k + 1) * CAP, :],
                (row_weight[k] * cot).astype(bf16),
                preferred_element_type=f32,
            ).astype(bf16)
        pl.semaphore_wait(barrier, len(partners))

        along = [
            send(held.at[z], held.at[z], e, other_z(j) * 2 + c) for j in range(1, depth)
        ]
        across = {}
        beside = []

        own_beside = []

        def came_from(i):
            return lax.rem(e - i + pieces, pieces)

        def products(piece, span):
            lines = pl.ds(pl.multiple_of(piece * width, 128), width)
            tok = rows[piece, 0]
            return (
                jnp.dot(tok, gate_v[lines, span], preferred_element_type=f32),
                jnp.dot(tok, up_v[lines, span], preferred_element_type=f32),
                lax.dot_general(
                    rows[piece, 1], down_v[span, lines], cols_t, preferred_element_type=f32
                ),
            )

        def first(t, carry):
            span = pl.ds(pl.multiple_of(t * unit_tile, unit_tile), unit_tile)
            for at, term in enumerate(products(e, span)):
                sums[at, :, span] = term
            return carry

        def place(zs):
            return pl.ds(pl.multiple_of((c * depth + zs) * CAP, CAP), CAP)

        def pass_on(j):
            zs = lax.rem(z - j + depth, depth)
            for i in range(1, pieces):
                across[j, i].wait_recv()
                spot = rows.at[came_from(i), :, place(zs), :]
                beside.append(send(spot, spot, e, z * 2 + 1 - c))

        for j in range(depth):
            zs = lax.rem(z - j + depth, depth)
            if j > 0:
                along[j - 1].wait_recv()
            for i in range(1, pieces):
                to_e = other_e(i)
                across[j, i] = send(
                    held.at[zs, to_e // per_expert], rows.at[e, :, place(zs), :], to_e, f
                )
            rows[e, :, place(zs), :] = held[zs, own]
            spot = rows.at[e, :, place(zs), :]
            own_beside.append(send(spot, spot, e, z * 2 + 1 - c))
            if j > 0:
                pass_on(j - 1)
        for load in loads:
            load.wait()
        for copy in own_beside:
            copy.wait_recv()
        lax.fori_loop(0, units // unit_tile, first, 0)
        pass_on(depth - 1)
        for copy in beside:
            copy.wait_recv()
        keep = pltpu.make_async_copy(rows, rows_out, load_sem.at[3 * pieces])
        keep.start()

        def forward(t, carry):
            span = pl.ds(pl.multiple_of(t * unit_tile, unit_tile), unit_tile)
            pre_gate, pre_up, grad_hidden = (sums[at, :, span] for at in range(3))
            for i in range(1, pieces):
                more = products(came_from(i), span)
                pre_gate += more[0]
                pre_up += more[1]
                grad_hidden += more[2]
            sig = jax.nn.sigmoid(pre_gate)
            activated = pre_gate * sig
            hid = activated * pre_up
            hid_ref[:, span] = hid.astype(bf16)
            hidt_ref[span, :] = hid.T.astype(bf16)
            dg_ref[:, span] = (
                grad_hidden * pre_up * (sig * (1.0 + pre_gate * (1.0 - sig)))
            ).astype(bf16)
            du_ref[:, span] = (grad_hidden * activated).astype(bf16)
            return carry

        lax.fori_loop(0, units // unit_tile, forward, 0)

        mine = pl.ds(pl.multiple_of(c * half, CAP), half)
        theirs = pl.ds(pl.multiple_of((1 - c) * half, CAP), half)
        pairs = []
        spreads = {}
        early = list(range(1, depth // 2 + 1))
        late = [j for j in range(depth) if j not in early and j > 0] + [0]

        def spread_out(i, j):
            to_e = other_e(i + 1)
            to_z = other_z(j)
            spreads[i, j] = send(
                parts.at[to_e, :, place(to_z), :],
                spread.at[e, :, pl.ds(pl.multiple_of(to_z * CAP, CAP), CAP), :],
                to_e,
                f,
            )

        def finish(i):
            to_e = other_e(i + 1)
            pairs[i].wait_recv()
            both = parts[to_e, :, mine, :].astype(f32) + paired[to_e].astype(f32)
            if i < pieces - 1:
                parts[to_e, :, mine, :] = both.astype(bf16)
                for j in early:
                    spread_out(i, j)
            else:
                spread[e] = both.astype(bf16)

        for i in range(pieces):
            to_e = other_e(i + 1)

            def backward(t, carry):
                spot = pl.ds(pl.multiple_of(t * col_tile, col_tile), col_tile)
                cols = pl.ds(pl.multiple_of(to_e * width + t * col_tile, 128), col_tile)
                parts[to_e, 0, :, spot] = jnp.dot(
                    hid_ref[...], down_v[:, cols], preferred_element_type=f32
                ).astype(bf16)
                back = lax.dot_general(
                    dg_ref[...], gate_v[cols, :], cols_t, preferred_element_type=f32
                )
                back += lax.dot_general(
                    du_ref[...], up_v[cols, :], cols_t, preferred_element_type=f32
                )
                parts[to_e, 1, :, spot] = back.astype(bf16)
                return carry

            lax.fori_loop(0, width // col_tile, backward, 0)
            pairs.append(
                send(parts.at[to_e, :, theirs, :], paired.at[to_e], e, z * 2 + 1 - c)
            )
            if i > 0:
                finish(i - 1)
        finish(pieces - 1)
        for j in late:
            for i in range(pieces - 1):
                spread_out(i, j)

        returns = []
        for j in early + late:
            for i in range(pieces - 1):
                spreads[i, j].wait_recv()
            to_z = other_z(j)
            span = pl.ds(pl.multiple_of(to_z * CAP, CAP), CAP)
            for k in range(WIN):
                total = 0.0
                for piece in range(k * per_expert, (k + 1) * per_expert):
                    total += spread[piece, :, span, :].astype(f32)
                if j > 0:
                    summed[j, k] = total.astype(bf16)
                else:
                    landed[z, k] = total.astype(bf16)
            if j > 0:
                returns.append(send(summed.at[j], landed.at[z], e, to_z * 2 + c))
        for copy in returns:
            copy.wait_recv()

        layer = jnp.zeros((group_rows, width), f32)
        back = jnp.zeros((group_rows, width), f32)
        for k in range(WIN):
            total = 0.0
            for zs in range(depth):
                total += landed[zs, k].astype(f32)
            total = total.astype(bf16)
            choice = pick_ref[k * CAP : (k + 1) * CAP, :]
            layer += row_weight[k] * lax.dot_general(
                choice, total[0], rows_t, preferred_element_type=f32
            )
            back += lax.dot_general(choice, total[1], rows_t, preferred_element_type=f32)
        layer_ref[...] = layer.astype(bf16)
        back_ref[...] = back.astype(bf16)
        for copy in started:
            copy.wait_send()
        keep.wait()

    vmem = pl.BlockSpec(memory_space=pltpu.VMEM)
    anywhere = pl.BlockSpec(memory_space=pl.ANY)
    shape = jax.ShapeDtypeStruct
    return pl.pallas_call(
        body,
        in_specs=[vmem] * 5 + [anywhere] * 3,
        out_specs=[vmem] * 5 + [anywhere],
        out_shape=[
            shape((group_rows, width), bf16),
            shape((group_rows, width), bf16),
            shape((units, slots), bf16),
            shape((slots, units), bf16),
            shape((slots, units), bf16),
            shape((pieces, 2, slots, width), bf16),
        ],
        scratch_shapes=[
            pltpu.VMEM(gate.shape, bf16),
            pltpu.VMEM(up.shape, bf16),
            pltpu.VMEM(down.shape, bf16),
            pltpu.VMEM((depth, WIN, 2, CAP, width), bf16),
            pltpu.VMEM((pieces, 2, slots, width), bf16),
            pltpu.VMEM((pieces, 2, slots, width), bf16),
            pltpu.VMEM((pieces, 2, half, width), bf16),
            pltpu.VMEM((pieces, 2, half, width), bf16),
            pltpu.VMEM((depth, WIN, 2, CAP, width), bf16),
            pltpu.VMEM((depth, WIN, 2, CAP, width), bf16),
            pltpu.VMEM((slots, units), bf16),
            pltpu.VMEM((3, slots, units), f32),
            pltpu.SemaphoreType.DMA((3 * pieces + 1,)),
            pltpu.SemaphoreType.DMA((n_copies,)),
            pltpu.SemaphoreType.DMA((n_copies,)),
        ],
        compiler_params=pltpu.CompilerParams(
            collective_id=0, has_side_effects=True, vmem_limit_bytes=62 * 1024 * 1024
        ),
        cost_estimate=pl.CostEstimate(
            flops=12 * slots * units * pieces * width,
            bytes_accessed=6 * units * pieces * width,
            transcendentals=slots * units,
        ),
    )(pick, ids, weights, tokens, cotangent, gate, up, down)


def local(tokens, cotangent, routed_experts, route_weights, gate, up, down):
    group_rows = tokens.shape[0]
    own_ids = lax.dynamic_slice_in_dim(
        routed_experts, lax.axis_index("fsdp") * group_rows, group_rows, 0
    )
    window = jnp.arange(WIN, dtype=jnp.int32)
    hits = own_ids[None] == window[:, None, None]
    member = jnp.any(hits, axis=2)
    earlier = jnp.triu(jnp.ones((group_rows, group_rows), jnp.bfloat16), 1)
    place = jnp.dot(member.astype(jnp.bfloat16), earlier, preferred_element_type=jnp.float32)
    chosen = member[:, None, :] & (
        place[:, None, :] == jnp.arange(CAP, dtype=jnp.float32)[None, :, None]
    )
    pick = chosen.astype(jnp.bfloat16).reshape(WIN * CAP, group_rows)
    layer, back, hidden_t, dgate, dup, rows = exchange_and_products(
        pick, own_ids, route_weights, tokens, cotangent, gate, up, down
    )
    dgates, dups, ddown = weight_grads(rows, hidden_t, dgate, dup)
    return layer, back, dgates, dups, ddown


def solution(mesh):
    columns = P(None, ("expert", "fsdp"))
    lines = P(("expert", "fsdp"), None)
    split = P("fsdp", "expert")
    return jax.shard_map(
        local,
        mesh=mesh,
        in_specs=(split, split, P(), P("fsdp", None), columns, columns, lines),
        out_specs=(split, split, columns, columns, lines),
        check_vma=False,
    )
```
